32 devices in a mesh: mem: 8 (over y, x, core), lat: 4 (over z).
Axes of the slice: x: 2, y: 2, z: 4, core: 2. Of those that a mesh axis runs over, the one named last changes fastest.
Arguments:
- perturb: bfloat16 [32, 4, 128, 1024], P('mem', None, 'lat'), may hold values from -16 to 16
- gradient: float32 [4, 128, 1024], P(None, 'lat', 'mem'), may hold values from -6 to 6
- k_north: float32 [4, 128, 1024], P(None, 'lat'), may hold values from 0.1 to 0.35
- k_east: float32 [4, 128, 1024], P(None, 'lat'), may hold values from 0.02 to 0.15
- scale: float32 [4, 128, 1024], P(None, 'lat'), may hold values from 0.25 to 1
Outputs:
- product: float32 [4, 128, 1024], P(None, 'lat', 'mem')
The draws below stay inside these ranges and needn't reach their ends.
All inputs are finite; a program needn't handle non-finite values.
Results may differ from the reference program's by a relative error of at most 0.0003.
Values sent between devices are 32-bit elements; how exact they have to be, the bound alone decides.
A program may use at most 128 MiB of HBM per device.

```python
import math
import jax
import jax.numpy as jnp
from jax import lax

MEM_DEV = 4
LEV = 4
LON = 1024
SWEEP = 4
MEMBERS = 32
LAT = 128
N_MEM = 8


def block_scale(stream_key, dims, cuts, low, high):
    def one(dim, parts):
        heights = jax.random.uniform(jax.random.fold_in(jax.random.fold_in(stream_key, 6), dim), (parts,), jnp.float32, low / len(cuts), high / len(cuts))
        return jnp.repeat(jnp.exp(heights), dims[dim] // parts).reshape((-1,) + (1,) * (len(dims) - dim - 1))

    level = one(*cuts[0])
    for cut in cuts[1:]:
        level = level * one(*cut)
    return level


def bell_draw(stream_key, extent, deviation, reach, shards=(), held_as=jnp.bfloat16):
    values = deviation * jax.random.normal(stream_key, extent, jnp.float32)
    if shards:
        values = values * block_scale(stream_key, extent, shards, -0.22, 0.18)
    return jnp.clip(values, -reach, reach).astype(held_as)


def setup_inputs(seed: int = 0) -> dict:
    arg_keys = jax.random.split(jax.random.key(seed), 6)
    perturb = bell_draw(arg_keys[0], (MEMBERS, LEV, LAT, LON), 4.0, 16.0, ((0, 8), (2, 4)))
    gradient = bell_draw(arg_keys[1], (LEV, LAT, LON), 1.0, 6.0, ((1, 4), (2, 8)), jnp.float32)
    k_north = jnp.clip(0.1 + 0.25 * jax.random.uniform(arg_keys[2], (LEV, LAT, LON), jnp.float32) ** block_scale(arg_keys[2], (LEV, LAT, LON), ((1, 4),), -0.2, 0.2), 0.1, 0.35)
    k_east = jnp.clip(0.02 + 0.13000001 * jax.random.uniform(arg_keys[3], (LEV, LAT, LON), jnp.float32) ** block_scale(arg_keys[3], (LEV, LAT, LON), ((1, 4),), -0.2, 0.2), 0.02, 0.15)
    scale = jnp.clip(jnp.exp(math.log(1.0) - 1.3862944 * jax.random.uniform(arg_keys[4], (LEV, LAT, LON), jnp.float32) ** block_scale(arg_keys[4], (LEV, LAT, LON), ((1, 4),), -0.2, 0.2)), 0.25, 1.0)
    return {"perturb": perturb, "gradient": gradient, "k_north": k_north, "k_east": k_east, "scale": scale}


def spread(values, k_north, k_east):
    middle = values[..., 1:-1, :]
    north_flux = k_north[:, 1:-1] * (values[..., 2:, :] - middle)
    south_flux = k_north[:, :-2] * (middle - values[..., :-2, :])
    east_face = k_east[:, 1:-1]
    east_flux = east_face * (jnp.roll(middle, -1, -1) - middle) - jnp.roll(east_face, 1, -1) * (middle - jnp.roll(middle, 1, -1))
    return north_flux - south_flux + east_flux


def pad_rows(array):
    widths = [(0, 0)] * (array.ndim - 2) + [(1, 1), (0, 0)]
    return jnp.pad(array, widths)


def reference(perturb, gradient, k_north, k_east, scale):
    row_total = k_north.shape[1]
    top_row = jnp.arange(row_total) == row_total - 1
    masked_north = jnp.where(top_row[None, :, None], jnp.float32(0.0), k_north)
    padded_north = pad_rows(masked_north)
    padded_east = pad_rows(k_east)
    padded_scale = pad_rows(scale)

    def member_block(running, block_data):
        member_data = block_data.astype(jnp.float32)
        field = member_data * gradient[None]
        for repeat in range(SWEEP):
            field = field + spread(pad_rows(field) * padded_scale, padded_north, padded_east)
        for repeat in range(SWEEP):
            field = field + scale * spread(pad_rows(field), padded_north, padded_east)
        return running + jnp.sum(member_data * field, axis=0), None

    blocks = perturb.reshape(N_MEM, MEM_DEV, perturb.shape[1], perturb.shape[2], perturb.shape[3])
    start_sum = jnp.zeros(gradient.shape, jnp.float32)
    running, unused = lax.scan(member_block, start_sum, blocks)
    return running / jnp.float32(MEM_DEV * N_MEM - 1)
```

```python
import functools

import jax
import jax.numpy as jnp
from jax import lax
from jax.experimental import pallas as pl
from jax.experimental.pallas import tpu as pltpu
from jax.sharding import PartitionSpec as P

SWEEP = 4
H = SWEEP


def twice(x):
    return jnp.concatenate([x, x], axis=-2)


def sweep_kernel(
    n, nz, fused, p_ref, g_ref, kn_ref, ke_ref, s_ref, out_ref,
    pt, kt, co, rs, ua, ub, uc, ud, gs, gall, part, rpart,
    ksend, krecv, usend, urecv, csend, crecv, gsend, grecv, psend, precv,
):
    members, levels, rows, lon = p_ref.shape
    groups = members // 2
    me = lax.axis_index("mem")
    z = lax.axis_index("lat")
    low, high = z > 0, z < nz - 1
    total = n * members
    width = gs.shape[-1]

    barrier = pltpu.get_barrier_semaphore()
    if fused:
        for d in range(1, n):
            pl.semaphore_signal(
                barrier, inc=1, device_id={"mem": lax.rem(me + d, n)},
                device_id_type=pl.DeviceIdType.MESH)

    @pl.when(low)
    def _():
        pl.semaphore_signal(barrier, inc=1, device_id={"lat": z - 1},
                            device_id_type=pl.DeviceIdType.MESH)

    @pl.when(high)
    def _():
        pl.semaphore_signal(barrier, inc=1, device_id={"lat": z + 1},
                            device_id_type=pl.DeviceIdType.MESH)

    gs[...] = jnp.swapaxes(g_ref[...], 0, 1)
    keep = jnp.logical_or(
        lax.broadcasted_iota(jnp.int32, (levels, rows, lon), 1) < rows - 1, high)
    kt[0, pl.ds(H, rows)] = jnp.swapaxes(jnp.where(keep, kn_ref[...], 0.0), 0, 1)
    kt[1, pl.ds(H, rows)] = jnp.swapaxes(ke_ref[...], 0, 1)
    kt[2, pl.ds(H, rows)] = jnp.swapaxes(s_ref[...], 0, 1)

    peers = (n - 1 if fused else 0) + low.astype(jnp.int32) + high.astype(jnp.int32)
    pl.semaphore_wait(barrier, peers)

    def halo(buf, sends, recvs, lead):
        at = lambda first: buf.at[:, pl.ds(first, H)] if lead else buf.at[pl.ds(first, H)]
        down = pltpu.make_async_remote_copy(
            src_ref=at(H), dst_ref=at(H + rows), send_sem=sends.at[0],
            recv_sem=recvs.at[0], device_id={"lat": z - 1},
            device_id_type=pl.DeviceIdType.MESH)
        up = pltpu.make_async_remote_copy(
            src_ref=at(rows), dst_ref=at(0), send_sem=sends.at[1],
            recv_sem=recvs.at[1], device_id={"lat": z + 1},
            device_id_type=pl.DeviceIdType.MESH)
        return down, up

    def start_halo(pair):
        pl.when(low)(pair[0].start)
        pl.when(high)(pair[1].start)

    def wait_sent(pair):
        pl.when(low)(pair[0].wait_send)
        pl.when(high)(pair[1].wait_send)

    khalo = halo(kt, ksend, krecv, True)
    uhalo = halo(ua, usend, urecv, False)
    chalo = halo(uc, csend, crecv, False)

    gcopies = []
    if fused:
        for d in range(1, n):
            peer = lax.rem(me + d, n)
            c = pltpu.make_async_remote_copy(
                src_ref=gs, dst_ref=gall.at[me], send_sem=gsend.at[d],
                recv_sem=grecv.at[d], device_id={"mem": peer},
                device_id_type=pl.DeviceIdType.MESH)
            c.start()
            gcopies.append(c)
        gall[me] = gs[...]
    start_halo(khalo)

    def blank(first):
        kt[0:2, first:first + H] = jnp.zeros((2, H, levels, lon), jnp.float32)
        kt[2, first:first + H] = jnp.ones((H, levels, lon), jnp.float32)
        ua[first:first + H] = jnp.zeros((H,) + ua.shape[1:], jnp.float32)
        uc[first:first + H] = jnp.zeros((H,) + uc.shape[1:], jnp.float32)

    pl.when(jnp.logical_not(low))(lambda: blank(0))
    pl.when(jnp.logical_not(high))(lambda: blank(H + rows))

    for half in range(rows // 16):
        block = p_ref[:, :, half * 16:(half + 1) * 16, :].astype(jnp.float32)
        block = block.reshape(members * levels, 16, lon)
        pt[half * 16:(half + 1) * 16] = jnp.swapaxes(block, 0, 1)

    def coefficient_row(r):
        kn, south = twice(kt[0, r]), twice(kt[0, r - 1])
        ke, s = twice(kt[1, r]), twice(kt[2, r])
        west = pltpu.roll(ke, 1, 1)
        co[0, r] = 1.0 - s * (kn + south + ke + west)
        co[1, r] = s * kn
        co[2, r] = s * south
        co[3, r] = s * ke
        co[4, r] = s * west
        rs[r] = 1.0 / s

    def each_row(first, last, body, block=4):
        count = last - first
        full = count // block

        def many(i, carry):
            for b in range(block):
                body(first + i * block + b)
            return carry

        if full:
            lax.fori_loop(0, full, many, 0)
        for r in range(first + full * block, last):
            body(r)

    each_row(H + 1, H + rows, coefficient_row)

    for c in gcopies:
        c.wait_recv()

    def start_row(r):
        if fused:
            g = jnp.concatenate([gall[b, r - H] for b in range(n)], axis=-1)
        else:
            g = gs[r - H]
        sg = twice(g * kt[2, r])
        for q in range(groups):
            ua[r, 8 * q:8 * q + 8] = pt[r - H, 8 * q:8 * q + 8] * sg

    each_row(H, 2 * H, start_row)
    each_row(rows, rows + H, start_row)
    start_halo(uhalo)
    each_row(2 * H, rows, start_row)

    def stepped(src, r):
        c0, cn, cs, ce, cw = (co[i, r] for i in range(5))
        result = []
        for q in range(groups):
            part_of = pl.ds(8 * q, 8)
            u = src[r, part_of]
            result.append(
                c0 * u + (cn * src[r + 1, part_of] + cs * src[r - 1, part_of])
                + (ce * pltpu.roll(u, lon - 1, 1) + cw * pltpu.roll(u, 1, 1)))
        return result

    def plain(src, dst, r):
        for q, v in enumerate(stepped(src, r)):
            dst[r, 8 * q:8 * q + 8] = v

    def unscaled(src, dst, r):
        inverse = rs[r]
        for q, v in enumerate(stepped(src, r)):
            dst[r, 8 * q:8 * q + 8] = v * inverse

    def product(src, dst, r):
        t = None
        for q, v in enumerate(stepped(src, r)):
            term = v * pt[r - H, 8 * q:8 * q + 8]
            t = term if t is None else t + term
        t = t[:levels] + t[levels:]
        if fused:
            for b in range(n):
                part[b, r - H] = t[:, b * width:(b + 1) * width]
        else:
            part[0, r - H] = t

    chain = [ub, ud] * SWEEP
    first_sweep, second_sweep = [], []
    for k in range(SWEEP):
        last = k == SWEEP - 1
        before = chain[k - 1]
        first_sweep.append(
            (ua if k == 0 else before, uc if last else chain[k], unscaled if last else plain))
        second_sweep.append(
            (uc if k == 0 else before, None if last else chain[k], product if last else plain))

    def inner(sweep):
        for k, (src, dst, fn) in enumerate(sweep):
            each_row(H + k + 1, H + rows - k - 1, functools.partial(fn, src, dst))

    def edge(sweep, upper):
        for k, (src, dst, fn) in enumerate(sweep):
            first = (rows + H - k - 1) if upper else k + 1
            each_row(first, first + H, functools.partial(fn, src, dst))

    inner(first_sweep)

    pl.when(high)(khalo[0].wait_recv)
    pl.when(low)(khalo[1].wait_recv)
    each_row(1, H + 1, coefficient_row)
    each_row(H + rows, H + rows + H - 1, coefficient_row)
    pl.when(high)(uhalo[0].wait_recv)
    pl.when(low)(uhalo[1].wait_recv)
    edge(first_sweep, False)
    pl.when(low)(chalo[0].start)
    edge(first_sweep, True)
    pl.when(high)(chalo[1].start)

    spans = ((H, rows - 2 * H), (0, H), (rows - H, H))
    pcopies = []

    def send_part(i):
        if not fused:
            return
        at, count = spans[i]
        for d in range(1, n):
            peer = lax.rem(me + d, n)
            c = pltpu.make_async_remote_copy(
                src_ref=part.at[peer, pl.ds(at, count)],
                dst_ref=rpart.at[d, pl.ds(at, count)],
                send_sem=psend.at[d, i], recv_sem=precv.at[d, i],
                device_id={"mem": peer}, device_id_type=pl.DeviceIdType.MESH)
            c.start()
            pcopies.append(c)

    inner(second_sweep)
    send_part(0)
    pl.when(low)(chalo[1].wait_recv)
    edge(second_sweep, False)
    send_part(1)
    pl.when(high)(chalo[0].wait_recv)
    edge(second_sweep, True)
    send_part(2)

    if fused:
        for c in pcopies:
            c.wait_recv()
        acc = part[me]
        for d in range(1, n):
            acc = acc + rpart[d]
        out_ref[...] = jnp.swapaxes(acc, 0, 1) / jnp.float32(total - 1)
    else:
        out_ref[...] = jnp.swapaxes(part[0], 0, 1) / jnp.float32(total - 1)

    for pair in (khalo, uhalo, chalo):
        wait_sent(pair)
    for c in gcopies:
        c.wait_send()
    for c in pcopies:
        c.wait_send()


def shards(n, nz, perturb, gradient, k_north, k_east, scale):
    members, levels, rows, lon = perturb.shape
    block = gradient.shape[2]
    fused = block % 128 == 0
    if not fused:
        gradient = lax.all_gather(gradient, "mem", axis=2, tiled=True)
    width = gradient.shape[2]
    units = members * levels
    f32 = jnp.float32
    blocks = n if fused else 1
    vmem = pl.BlockSpec(memory_space=pltpu.VMEM)
    out = pl.pallas_call(
        functools.partial(sweep_kernel, n, nz, fused),
        out_shape=jax.ShapeDtypeStruct((levels, rows, width), f32),
        in_specs=[vmem] * 5,
        out_specs=vmem,
        scratch_shapes=[
            pltpu.VMEM((rows, units, lon), f32),
            pltpu.VMEM((3, rows + 2 * H, levels, lon), f32),
            pltpu.VMEM((5, rows + 2 * H, 2 * levels, lon), f32),
            pltpu.VMEM((rows + 2 * H, 2 * levels, lon), f32),
            pltpu.VMEM((rows + 2 * H, units, lon), f32),
            pltpu.VMEM((rows + 2 * H, units, lon), f32),
            pltpu.VMEM((rows + 2 * H, units, lon), f32),
            pltpu.VMEM((rows + 2 * H, units, lon), f32),
            pltpu.VMEM((rows, levels, width), f32),
            pltpu.VMEM((blocks, rows, levels, width), f32),
            pltpu.VMEM((blocks, rows, levels, width), f32),
            pltpu.VMEM((blocks, rows, levels, width), f32),
            pltpu.SemaphoreType.DMA((2,)),
            pltpu.SemaphoreType.DMA((2,)),
            pltpu.SemaphoreType.DMA((2,)),
            pltpu.SemaphoreType.DMA((2,)),
            pltpu.SemaphoreType.DMA((2,)),
            pltpu.SemaphoreType.DMA((2,)),
            pltpu.SemaphoreType.DMA((n,)),
            pltpu.SemaphoreType.DMA((n,)),
            pltpu.SemaphoreType.DMA((n, 3)),
            pltpu.SemaphoreType.DMA((n, 3)),
        ],
        compiler_params=pltpu.CompilerParams(
            collective_id=0, has_side_effects=True, vmem_limit_bytes=48 * 1024 * 1024),
    )(perturb, gradient, k_north, k_east, scale)
    if not fused:
        out = lax.psum_scatter(out, "mem", scatter_dimension=2, tiled=True)
    return out


def solution(mesh):
    placed = (
        P("mem", None, "lat", None),
        P(None, "lat", "mem"),
        P(None, "lat", None),
        P(None, "lat", None),
        P(None, "lat", None),
    )
    return jax.shard_map(
        functools.partial(shards, mesh.shape["mem"], mesh.shape["lat"]),
        mesh=mesh, in_specs=placed, out_specs=P(None, "lat", "mem"), check_vma=False)
```

```python
import functools

import jax
import jax.numpy as jnp
from jax import lax
from jax.experimental import pallas as pl
from jax.experimental.pallas import tpu as pltpu
from jax.sharding import PartitionSpec as P

SWEEP = 4
H = SWEEP


def twice(x):
    return jnp.concatenate([x, x], axis=-2)


def shuffled(x, order, dims):
    total = None
    for _ in range(2):
        piece = x.astype(jnp.bfloat16)
        moved = lax.dot_general(piece, order, (dims, ((), ())),
                                preferred_element_type=jnp.float32)
        total = moved if total is None else total + moved
        x = x - piece.astype(jnp.float32)
    return total


def sweep_kernel(
    n, nz, fused, p_ref, g_ref, kn_ref, ke_ref, s_ref, out_ref,
    pt, kt, co, rs, ua, ub, uc, ud, order, gp, sums, gs, gall, part, spart, comb, rpart,
    ksend, krecv, usend, urecv, csend, crecv, gsend, grecv, psend, precv,
):
    members, levels, rows, lon = p_ref.shape
    groups = members // 2
    me = lax.axis_index("mem")
    z = lax.axis_index("lat")
    low, high = z > 0, z < nz - 1
    total = n * members
    width = gs.shape[-1]

    barrier = pltpu.get_barrier_semaphore()
    if fused:
        for d in range(1, n):
            pl.semaphore_signal(
                barrier, inc=1, device_id={"mem": lax.rem(me + d, n)},
                device_id_type=pl.DeviceIdType.MESH)

    @pl.when(low)
    def _():
        pl.semaphore_signal(barrier, inc=1, device_id={"lat": z - 1},
                            device_id_type=pl.DeviceIdType.MESH)

    @pl.when(high)
    def _():
        pl.semaphore_signal(barrier, inc=1, device_id={"lat": z + 1},
                            device_id_type=pl.DeviceIdType.MESH)

    chunks = lon // 128

    offset = (lax.broadcasted_iota(jnp.int32, (128, 128), 0)
              - chunks * lax.broadcasted_iota(jnp.int32, (128, 128), 1))

    def order_rows(i, carry):
        row = pl.ds(pl.multiple_of(i * 128, 128), 128)
        for c in range(chunks):
            order[row, c * 128:c * 128 + 128] = jnp.where(
                offset == c - i * 128, 1.0, 0.0).astype(jnp.bfloat16)
        return carry

    gs[...] = jnp.swapaxes(g_ref[...], 0, 1)
    lax.fori_loop(0, chunks, order_rows, 0)

    def east(x):
        return jnp.concatenate([x[:, 128:], pltpu.roll(x[:, :128], 127, 1)], axis=1)

    def west_of(x):
        return jnp.concatenate([pltpu.roll(x[:, lon - 128:], 1, 1), x[:, :lon - 128]], axis=1)

    block = p_ref[...].reshape(members * levels * rows, lon)
    block = jnp.dot(block, order[...], preferred_element_type=jnp.float32)
    pt[...] = jnp.swapaxes(block.reshape(members * levels, rows, lon), 0, 1)

    peers = (n - 1 if fused else 0) + low.astype(jnp.int32) + high.astype(jnp.int32)
    pl.semaphore_wait(barrier, peers)

    def halo(at, sends, recvs, q):
        down = pltpu.make_async_remote_copy(
            src_ref=at(H), dst_ref=at(H + rows), send_sem=sends.at[0, q],
            recv_sem=recvs.at[0, q], device_id={"lat": z - 1},
            device_id_type=pl.DeviceIdType.MESH)
        up = pltpu.make_async_remote_copy(
            src_ref=at(rows), dst_ref=at(0), send_sem=sends.at[1, q],
            recv_sem=recvs.at[1, q], device_id={"lat": z + 1},
            device_id_type=pl.DeviceIdType.MESH)
        return down, up

    def start_halo(pair):
        pl.when(low)(pair[0].start)
        pl.when(high)(pair[1].start)

    def wait_halo(pair):
        pl.when(high)(pair[0].wait_recv)
        pl.when(low)(pair[1].wait_recv)

    def wait_sent(pair):
        pl.when(low)(pair[0].wait_send)
        pl.when(high)(pair[1].wait_send)

    def unit_rows(buf, q):
        return lambda first: buf.at[pl.ds(first, H), pl.ds(8 * q, 8)]

    khalo = halo(lambda first: kt.at[:, pl.ds(first, H)], ksend, krecv, 0)
    uhalo = [halo(unit_rows(ua, q), usend, urecv, q) for q in range(groups)]
    chalo = [halo(unit_rows(uc, q), csend, crecv, q) for q in range(groups)]

    chips, chip, core = n // 2, me // 2, lax.rem(me, 2)
    sibling = 2 * chip + 1 - core

    def remote(src, dst, ssem, rsem, mem):
        return pltpu.make_async_remote_copy(
            src_ref=src, dst_ref=dst, send_sem=ssem, recv_sem=rsem,
            device_id={"mem": mem}, device_id_type=pl.DeviceIdType.MESH)

    def chip_at(d):
        return lax.rem(chip + d, chips)

    gcopies, forwards = [], []
    if fused:
        for d in range(1, chips):
            gcopies.append(remote(gs, gall.at[me], gsend.at[d], grecv.at[d],
                                  2 * chip_at(d) + core))
        forwards.append(remote(gs, gall.at[me], gsend.at[0], grecv.at[0], sibling))
        for c in gcopies + forwards:
            c.start()
        gall[me] = gs[...]

    keep = jnp.logical_or(
        lax.broadcasted_iota(jnp.int32, (levels, rows, lon), 1) < rows - 1, high)
    three = jnp.concatenate(
        [jnp.where(keep, kn_ref[...], 0.0), ke_ref[...], s_ref[...]], axis=0)
    three = shuffled(three.reshape(3 * levels * rows, lon), order[...], ((1,), (0,)))
    three = three.reshape(3, levels, rows, lon)
    for i in range(3):
        kt[i, pl.ds(H, rows)] = jnp.swapaxes(three[i], 0, 1)
    start_halo(khalo)
    for d, c in enumerate(gcopies, 1):
        c.wait_recv()
        at = gall.at[2 * chip_at(chips - d) + core]
        c = remote(at, at, gsend.at[chips + d], grecv.at[chips + d], sibling)
        c.start()
        forwards.append(c)

    def blank(first):
        kt[0:2, first:first + H] = jnp.zeros((2, H, levels, lon), jnp.float32)
        kt[2, first:first + H] = jnp.ones((H, levels, lon), jnp.float32)
        ua[first:first + H] = jnp.zeros((H,) + ua.shape[1:], jnp.float32)
        uc[first:first + H] = jnp.zeros((H,) + uc.shape[1:], jnp.float32)

    pl.when(jnp.logical_not(low))(lambda: blank(0))
    pl.when(jnp.logical_not(high))(lambda: blank(H + rows))

    def coefficient_row(r):
        kn, south = twice(kt[0, r]), twice(kt[0, r - 1])
        ke, s = twice(kt[1, r]), twice(kt[2, r])
        west = west_of(ke)
        co[0, r] = 1.0 - s * (kn + south + ke + west)
        co[1, r] = s * kn
        co[2, r] = s * south
        co[3, r] = s * ke
        co[4, r] = s * west
        rs[r] = 1.0 / s

    def each_row(first, last, body, block=4):
        count = last - first
        full = count // block

        def many(i, carry):
            for b in range(block):
                body(first + i * block + b)
            return carry

        if full:
            lax.fori_loop(0, full, many, 0)
        for r in range(first + full * block, last):
            body(r)

    each_row(H + 1, H + rows, coefficient_row)

    for c in forwards:
        c.wait_recv()

    if fused:
        g = jnp.concatenate([gall[b] for b in range(n)], axis=-1)
    else:
        g = gs[...]
    gp[...] = shuffled(g.reshape(rows * levels, lon), order[...], ((1,), (0,))).reshape(
        rows, levels, lon)

    def start_row(r):
        sg = twice(gp[r - H] * kt[2, r])
        for q in range(groups):
            ua[r, 8 * q:8 * q + 8] = pt[r - H, 8 * q:8 * q + 8] * sg

    each_row(H, 2 * H, start_row)
    each_row(rows, rows + H, start_row)
    for pair in uhalo:
        start_halo(pair)
    each_row(2 * H, rows, start_row)

    def stepped(src, r, q):
        c0, cn, cs, ce, cw = (co[i, r] for i in range(5))
        part_of = pl.ds(8 * q, 8)
        u = src[r, part_of]
        return (c0 * u + (cn * src[r + 1, part_of] + cs * src[r - 1, part_of])
                + (ce * east(u) + cw * west_of(u)))

    def plain(src, dst, q, r):
        dst[r, 8 * q:8 * q + 8] = stepped(src, r, q)

    def unscaled(src, dst, q, r):
        dst[r, 8 * q:8 * q + 8] = stepped(src, r, q) * rs[r]

    def product(src, dst, q, r):
        t = stepped(src, r, q) * pt[r - H, 8 * q:8 * q + 8]
        t = t[:levels] + t[levels:]
        sums[r - H] = t if q == 0 else sums[r - H] + t

    chain = [ub, ud] * SWEEP
    first_sweep, second_sweep = [], []
    for k in range(SWEEP):
        last = k == SWEEP - 1
        before = chain[k - 1]
        first_sweep.append(
            (ua if k == 0 else before, uc if last else chain[k], unscaled if last else plain))
        second_sweep.append(
            (uc if k == 0 else before, None if last else chain[k], product if last else plain))

    def inner(sweep, q):
        for k, (src, dst, fn) in enumerate(sweep):
            each_row(H + k + 1, H + rows - k - 1, functools.partial(fn, src, dst, q), 8)

    def edge(sweep, q):
        for k, (src, dst, fn) in enumerate(sweep):
            for first in (k + 1, rows + H - k - 1):
                for r in range(first, first + H):
                    fn(src, dst, q, r)

    for q in range(groups):
        inner(first_sweep, q)
        if q == 0:
            wait_halo(khalo)
            for r in (*range(1, H + 1), *range(H + rows, 2 * H + rows - 1)):
                coefficient_row(r)
        wait_halo(uhalo[q])
        edge(first_sweep, q)
        start_halo(chalo[q])

    spans = ((H, rows - 2 * H), (0, H), (rows - H, H))
    pairs, pcopies = {}, []

    def pair_part(i):
        at, count = spans[i]
        t = sums[at:at + count].reshape(count * levels, lon)
        t = shuffled(t, order[...], ((1,), (1,))).reshape(count, levels, lon)
        if not fused:
            part[0, 0, at:at + count] = t
            return
        for b in range(n):
            part[b % 2, b // 2, at:at + count] = t[:, :, b * width:(b + 1) * width]
        rows_of = pl.ds(at, count)
        pairs[i] = remote(part.at[1 - core, :, rows_of], spart.at[:, rows_of],
                          psend.at[0, i], precv.at[0, i], sibling)
        pairs[i].start()

    def send_part(i):
        if not fused:
            return
        at, count = spans[i]
        rows_of = pl.ds(at, count)
        pairs[i].wait_recv()
        comb[:, at:at + count] = part[core, :, rows_of] + spart[:, at:at + count]
        for d in range(1, chips):
            c = remote(comb.at[chip_at(d), rows_of], rpart.at[d, rows_of],
                       psend.at[d, i], precv.at[d, i], 2 * chip_at(d) + core)
            c.start()
            pcopies.append(c)

    for q in range(groups):
        inner(second_sweep, q)
        if q == groups - 1:
            pair_part(0)
        wait_halo(chalo[q])
        edge(second_sweep, q)
    send_part(0)
    for i in (1, 2):
        pair_part(i)
    for i in (1, 2):
        send_part(i)

    if fused:
        for c in pcopies:
            c.wait_recv()
        acc = comb[chip]
        for d in range(1, chips):
            acc = acc + rpart[d]
        out_ref[...] = jnp.swapaxes(acc, 0, 1) / jnp.float32(total - 1)
    else:
        out_ref[...] = jnp.swapaxes(part[0, 0], 0, 1) / jnp.float32(total - 1)

    for pair in (khalo, *uhalo, *chalo):
        wait_sent(pair)
    for c in (*gcopies, *forwards, *pairs.values(), *pcopies):
        c.wait_send()


def shards(n, nz, perturb, gradient, k_north, k_east, scale):
    members, levels, rows, lon = perturb.shape
    block = gradient.shape[2]
    fused = block % 128 == 0
    if not fused:
        gradient = lax.all_gather(gradient, "mem", axis=2, tiled=True)
    width = gradient.shape[2]
    units = members * levels
    f32 = jnp.float32
    blocks, cores = (n, 2) if fused else (1, 1)
    vmem = pl.BlockSpec(memory_space=pltpu.VMEM)
    out = pl.pallas_call(
        functools.partial(sweep_kernel, n, nz, fused),
        out_shape=jax.ShapeDtypeStruct((levels, rows, width), f32),
        in_specs=[vmem] * 5,
        out_specs=vmem,
        scratch_shapes=[
            pltpu.VMEM((rows, units, lon), f32),
            pltpu.VMEM((3, rows + 2 * H, levels, lon), f32),
            pltpu.VMEM((5, rows + 2 * H, 2 * levels, lon), f32),
            pltpu.VMEM((rows + 2 * H, 2 * levels, lon), f32),
            pltpu.VMEM((rows + 2 * H, units, lon), f32),
            pltpu.VMEM((rows + 2 * H, units, lon), f32),
            pltpu.VMEM((rows + 2 * H, units, lon), f32),
            pltpu.VMEM((rows + 2 * H, units, lon), f32),
            pltpu.VMEM((lon, lon), jnp.bfloat16),
            pltpu.VMEM((rows, levels, lon), f32),
            pltpu.VMEM((rows, levels, lon), f32),
            pltpu.VMEM((rows, levels, width), f32),
            pltpu.VMEM((blocks, rows, levels, width), f32),
            pltpu.VMEM((cores, blocks // cores, rows, levels, width), f32),
            pltpu.VMEM((blocks // cores, rows, levels, width), f32),
            pltpu.VMEM((blocks // cores, rows, levels, width), f32),
            pltpu.VMEM((blocks // cores, rows, levels, width), f32),
            pltpu.SemaphoreType.DMA((2, 1)),
            pltpu.SemaphoreType.DMA((2, 1)),
            pltpu.SemaphoreType.DMA((2, members // 2)),
            pltpu.SemaphoreType.DMA((2, members // 2)),
            pltpu.SemaphoreType.DMA((2, members // 2)),
            pltpu.SemaphoreType.DMA((2, members // 2)),
            pltpu.SemaphoreType.DMA((n,)),
            pltpu.SemaphoreType.DMA((n,)),
            pltpu.SemaphoreType.DMA((n, 3)),
            pltpu.SemaphoreType.DMA((n, 3)),
        ],
        compiler_params=pltpu.CompilerParams(
            collective_id=0, has_side_effects=True, vmem_limit_bytes=48 * 1024 * 1024),
    )(perturb, gradient, k_north, k_east, scale)
    if not fused:
        out = lax.psum_scatter(out, "mem", scatter_dimension=2, tiled=True)
    return out


def solution(mesh):
    placed = (
        P("mem", None, "lat", None),
        P(None, "lat", "mem"),
        P(None, "lat", None),
        P(None, "lat", None),
        P(None, "lat", None),
    )
    return jax.shard_map(
        functools.partial(shards, mesh.shape["mem"], mesh.shape["lat"]),
        mesh=mesh, in_specs=placed, out_specs=P(None, "lat", "mem"), check_vma=False)
```
